512 devices in a mesh: row: 16 (over y, core), col: 8 (over z), depth: 4 (over x).
Axes of the slice: x: 4, y: 8, z: 8, core: 2. Of those that a mesh axis runs over, the one named last changes fastest.
Arguments:
- density: float32 [512, 5, 128, 128], P(('row', 'depth'), None, 'col'), may hold values from -0.6 to 0.6
- pattern: int32 [512, 5], P(('row', 'depth')), may hold values 0 or 1
Outputs:
- purified: float32 [512, 5, 128, 128], P(('row', 'depth'), None, 'col')
The draws below stay inside these ranges and needn't reach their ends.
All inputs are finite; a program needn't handle non-finite values. No bound on the sum of `pattern` on one device may be relied on, other than what follows from the above.
Results may differ from the reference program's by a relative error of at most 0.0001.
Values sent between devices are 32-bit elements; how exact they have to be, the bound alone decides.
No kernel may reach another device: no remote copies, remote signals or barrier semaphores. Data moves between devices by JAX's collectives and lax.ppermute only.
A program may use at most 64 MiB of HBM per device.

```python
import jax
import jax.numpy as jnp
from jax import lax

BLOCK = 128
HALF = 2
BLOCKS = 512
WIDE = 5


def with_ends(drawn, key, low, high):
    place = [jax.random.randint(jax.random.fold_in(key, axis), (), 0, length) for axis, length in enumerate(drawn.shape)]
    main_axis = drawn.shape.index(max(drawn.shape))
    neighbour = place[:main_axis] + [(place[main_axis] + 1) % drawn.shape[main_axis]] + place[main_axis + 1:]
    return drawn.at[tuple(place)].set(low).at[tuple(neighbour)].set(high)


def shard_levels(own_key, extent, pieces, smallest, top_value):
    def one(dim, shards_of):
        heights = jax.random.uniform(jax.random.fold_in(jax.random.fold_in(own_key, 6), dim), (shards_of,), jnp.float32, smallest / len(pieces), top_value / len(pieces))
        return jnp.repeat(jnp.exp(heights), extent[dim] // shards_of).reshape((-1,) + (1,) * (len(extent) - dim - 1))

    gain = one(*pieces[0])
    for cut in pieces[1:]:
        gain = gain * one(*cut)
    return gain


def bell_draw(key, dims, deviation, reach, shards=(), dtype=jnp.bfloat16):
    entries = jax.random.normal(key, dims, jnp.float32) * deviation
    if len(shards) > 0:
        entries = shard_levels(key, dims, shards, -0.22, 0.18) * entries
    return jnp.clip(entries, min=-reach, max=reach).astype(dtype)


def setup_inputs(seed: int = 0) -> dict:
    key_list = jax.random.split(jax.random.key(seed), 3)
    density = bell_draw(key_list[0], (BLOCKS, WIDE, BLOCK, BLOCK), 0.1, 0.6, ((0, 64), (2, 8)), jnp.float32)
    pattern = with_ends((jax.random.randint(key_list[1], (BLOCKS, WIDE), 0, 4) < 3).astype(jnp.int32), jax.random.fold_in(key_list[1], 1), 0, 1)
    return dict(density=density, pattern=pattern)


def banded_product(left_tiles, other_tiles, pattern):
    summed = jnp.zeros(left_tiles.shape, jnp.float32)
    for source in range(WIDE):
        first_slot = max(0, source - HALF)
        last_slot = min(WIDE, source + HALF + 1)
        shifted = jnp.roll(other_tiles, -(source - HALF), axis=0)
        partner = shifted[:, first_slot - source + HALF:last_slot - source + HALF]
        contrib = jnp.einsum("iab,itbc->itac", left_tiles[:, source], partner, precision=lax.Precision.HIGHEST)
        summed = summed.at[:, first_slot:last_slot].add(contrib)
    return summed * pattern[:, :, None, None].astype(jnp.float32)


def reference(density, pattern):
    masked = density * pattern[:, :, None, None].astype(jnp.float32)
    square = banded_product(masked, masked, pattern)
    cube = banded_product(square, masked, pattern)
    return 3.0 * square - 2.0 * cube
```

```python
import jax
import jax.numpy as jnp
from jax import lax
from jax.experimental import pallas as pl
from jax.experimental.pallas import tpu as pltpu
from jax.sharding import PartitionSpec as P

HALF = 2
WIDE = 5
AXES = ("row", "col", "depth")


def ring_pairs(sizes, shift):
    rows, cols, depths = sizes
    total = rows * cols * depths

    def place(i):
        chunk, col = divmod(i % total, cols)
        row, depth = divmod(chunk, depths)
        return (row * cols + col) * depths + depth

    return [(place(i + shift), place(i)) for i in range(total)]


def halves(value):
    high = value.astype(jnp.bfloat16)
    return high, (value - high.astype(jnp.float32)).astype(jnp.bfloat16)


def dot(left, right):
    return jnp.dot(left, right, preferred_element_type=jnp.float32)


def band_kernel(pattern_ref, own_ref, m2_ref, m1_ref, p1_ref, p2_ref, out_ref):
    stored = (m2_ref, m1_ref, own_ref, p1_ref, p2_ref)
    first = (2, 1, 0, 0, 0)
    right = {}
    for u in range(WIDE):
        for s in range(stored[u].shape[0]):
            right[u, s + first[u]] = halves(stored[u][s])
    keep = [pattern_ref[t].astype(jnp.float32) for t in range(WIDE)]

    def product(left):
        result = []
        for t in range(WIDE):
            summed = None
            for u in range(max(0, t - HALF), min(WIDE, t + HALF + 1)):
                high, low = left[u]
                other_high, other_low = right[u, t - u + HALF]
                term = dot(high, other_high) + dot(high, other_low) + dot(low, other_high)
                summed = term if summed is None else summed + term
            result.append(summed * keep[t])
        return result

    square = product([right[HALF, s] for s in range(WIDE)])
    cube = product([halves(block) for block in square])
    for t in range(WIDE):
        out_ref[:, t] = (3.0 * square[t] - 2.0 * cube[t]).reshape(out_ref.shape[0], -1, out_ref.shape[3])


def shards(density, pattern):
    sizes = tuple(lax.axis_size(a) for a in AXES)
    cols, wide, rows, width = density.shape
    keep = lax.dynamic_index_in_dim(pattern, lax.axis_index("col"), 0, keepdims=False)
    parts = lax.all_to_all(density, "col", 0, 0, tiled=True)
    own = jnp.swapaxes(parts, 0, 1) * keep.astype(jnp.float32)[:, None, None, None]
    own = own.reshape(wide, cols * rows, width)
    p1 = lax.ppermute(own[:4], AXES, ring_pairs(sizes, 1))
    m1 = lax.ppermute(own[1:], AXES, ring_pairs(sizes, -1))
    p2 = lax.ppermute(own[:3], AXES, ring_pairs(sizes, 2))
    m2 = lax.ppermute(own[2:], AXES, ring_pairs(sizes, -2))
    vmem = pl.BlockSpec(memory_space=pltpu.VMEM)
    result = pl.pallas_call(
        band_kernel,
        out_shape=jax.ShapeDtypeStruct(density.shape, jnp.float32),
        in_specs=[pl.BlockSpec(memory_space=pltpu.SMEM)] + [vmem] * 5,
        out_specs=vmem,
        compiler_params=pltpu.CompilerParams(vmem_limit_bytes=32 * 1024 * 1024),
    )(keep, own, m2, m1, p1, p2)
    return lax.all_to_all(result, "col", 0, 0, tiled=True)


def solution(mesh):
    in_specs = (P(("row", "depth"), None, "col", None), P(("row", "depth"), None))
    out_specs = P(("row", "depth"), None, "col", None)
    return jax.shard_map(shards, mesh=mesh, in_specs=in_specs, out_specs=out_specs, check_vma=False)
```

```python
import jax
import jax.numpy as jnp
from jax import lax
from jax.experimental import pallas as pl
from jax.experimental.pallas import tpu as pltpu
from jax.sharding import PartitionSpec as P

HALF = 2
WIDE = 5
AXES = ("row", "col", "depth")


def place(sizes, i):
    rows, cols, depths = sizes
    chunk, col = divmod(i % (rows * cols * depths), cols)
    row, depth = divmod(chunk, depths)
    return (row * cols + (cols - 1 - col if chunk % 2 else col)) * depths + depth


def ring_pairs(sizes, shift):
    total = sizes[0] * sizes[1] * sizes[2]
    return [(place(sizes, i + shift), place(sizes, i)) for i in range(total)]


def halves(value):
    high = value.astype(jnp.bfloat16)
    return high, (value - high.astype(jnp.float32)).astype(jnp.bfloat16)


def dot(left, right):
    return jnp.dot(left, right, preferred_element_type=jnp.float32)


def band_kernel(turn_ref, pattern_ref, own_ref, m2_ref, m1_ref, p1_ref, p2_ref, out_ref):
    parts, _, rows, _ = out_ref.shape
    stored = (m2_ref, m1_ref, own_ref, p1_ref, p2_ref)
    first = (2, 1, 0, 0, 0)
    right = {}
    for u in range(WIDE):
        for s in range(stored[u].shape[0]):
            right[u, s + first[u]] = halves(stored[u][s])
    keep = [pattern_ref[t].astype(jnp.float32) for t in range(WIDE)]

    def product(left):
        result = []
        for t in range(WIDE):
            summed = None
            for u in range(max(0, t - HALF), min(WIDE, t + HALF + 1)):
                high, low = left[u]
                other_high, other_low = right[u, t - u + HALF]
                term = dot(high, other_high) + dot(high, other_low) + dot(low, other_high)
                summed = term if summed is None else summed + term
            result.append(summed * keep[t])
        return result

    square = product([right[HALF, s] for s in range(WIDE)])
    cube = product([halves(block) for block in square])
    for t in range(WIDE):
        value = 3.0 * square[t] - 2.0 * cube[t]
        for part in range(parts):
            out_ref[part ^ turn_ref[0], t] = value[part * rows : (part + 1) * rows]


def shards(density, pattern):
    sizes = tuple(lax.axis_size(a) for a in AXES)
    cols, wide, rows, width = density.shape
    groups = [[place(sizes, i + j) for j in range(cols)] for i in range(0, sizes[0] * sizes[1] * sizes[2], cols)]
    turned = (lax.axis_index("row") * sizes[2] + lax.axis_index("depth")) % 2
    turn = turned * (cols - 1)
    keep = lax.dynamic_index_in_dim(pattern, lax.axis_index("col") ^ turn, 0, keepdims=False)
    parts = lax.all_to_all(density, AXES, 0, 0, axis_index_groups=groups, tiled=True)
    parts = jnp.where(turned == 1, jnp.flip(parts, 0), parts)
    own = jnp.swapaxes(parts, 0, 1) * keep.astype(jnp.float32)[:, None, None, None]
    own = own.reshape(wide, cols * rows, width)
    p1 = lax.ppermute(own[:4], AXES, ring_pairs(sizes, 1))
    m1 = lax.ppermute(own[1:], AXES, ring_pairs(sizes, -1))
    p2 = lax.ppermute(own[:3], AXES, ring_pairs(sizes, 2))
    m2 = lax.ppermute(own[2:], AXES, ring_pairs(sizes, -2))
    vmem = pl.BlockSpec(memory_space=pltpu.VMEM)
    result = pl.pallas_call(
        band_kernel,
        out_shape=jax.ShapeDtypeStruct(density.shape, jnp.float32),
        in_specs=[pl.BlockSpec(memory_space=pltpu.SMEM)] * 2 + [vmem] * 5,
        out_specs=vmem,
        compiler_params=pltpu.CompilerParams(vmem_limit_bytes=32 * 1024 * 1024),
    )(turn.reshape(1), keep, own, m2, m1, p1, p2)
    return lax.all_to_all(result, AXES, 0, 0, axis_index_groups=groups, tiled=True)


def solution(mesh):
    in_specs = (P(("row", "depth"), None, "col", None), P(("row", "depth"), None))
    out_specs = P(("row", "depth"), None, "col", None)
    return jax.shard_map(shards, mesh=mesh, in_specs=in_specs, out_specs=out_specs, check_vma=False)
```

```python
import jax
import jax.numpy as jnp
from jax import lax
from jax.experimental import pallas as pl
from jax.experimental.pallas import tpu as pltpu
from jax.sharding import PartitionSpec as P

HALF = 2
WIDE = 5
AXES = ("row", "col", "depth")
VMEM = pl.BlockSpec(memory_space=pltpu.VMEM)
PARAMS = pltpu.CompilerParams(vmem_limit_bytes=32 * 1024 * 1024)


def owner(sizes, i):
    rows, cols, depths = sizes
    chunk, col = divmod(i % (rows * cols * depths), cols)
    row, depth = divmod(chunk, depths)
    return (row * cols + (cols - 1 - col if chunk % 2 else col)) * depths + depth


def exchange(sizes, first):
    result = []
    for i in range(first, sizes[0] * sizes[1] * sizes[2], 2):
        a, b = owner(sizes, i), owner(sizes, i + 1)
        result += [(a, b), (b, a)]
    return result


def place():
    chunk = lax.axis_index("row") * lax.axis_size("depth") + lax.axis_index("depth")
    flip = (chunk & 1) * (lax.axis_size("col") - 1)
    return flip, lax.axis_index("col") ^ flip


def halves(value):
    high = value.astype(jnp.bfloat16)
    return high, (value - high.astype(jnp.float32)).astype(jnp.bfloat16)


def dot(left, right):
    return jnp.dot(left, right, preferred_element_type=jnp.float32)


def arrange_kernel(marks_ref, parts_ref, own_ref, near_ref, far_ref):
    parts, _, rows, _ = parts_ref.shape
    flip, row = place()
    odd = row & 1
    for slot in range(WIDE):
        keep = marks_ref[pl.ds(row, 1), slot : slot + 1]
        for part in range(parts):
            own_ref[slot, part * rows : (part + 1) * rows] = parts_ref[part ^ flip, slot] * keep
    for slot in range(WIDE - 1):
        near_ref[slot] = own_ref[slot + 1 - odd]
        far_ref[slot] = own_ref[slot + odd]


def band_kernel(marks_ref, own_ref, near_ref, far_ref, relayed_ref, handed_ref, out_ref):
    parts, _, rows, _ = out_ref.shape
    flip, row = place()
    even = row & 1 == 0
    right = {(HALF, s): halves(own_ref[s]) for s in range(WIDE)}
    for s in range(WIDE - 1):
        near, far = near_ref[s], far_ref[s]
        right[HALF + 1, s] = halves(jnp.where(even, near, far))
        right[HALF - 1, s + 1] = halves(jnp.where(even, far, near))
    for s in range(WIDE - 2):
        relayed, handed = relayed_ref[s], handed_ref[s]
        right[HALF + 2, s] = halves(jnp.where(even, handed, relayed))
        right[HALF - 2, s + 2] = halves(jnp.where(even, relayed, handed))
    keep = [marks_ref[pl.ds(row, 1), t : t + 1] for t in range(WIDE)]

    def product(left):
        result = []
        for t in range(WIDE):
            summed = None
            for u in range(max(0, t - HALF), min(WIDE, t + HALF + 1)):
                high, low = left[u]
                other_high, other_low = right[u, t - u + HALF]
                term = dot(high, other_high) + dot(high, other_low) + dot(low, other_high)
                summed = term if summed is None else summed + term
            result.append(summed * keep[t])
        return result

    square = product([right[HALF, s] for s in range(WIDE)])
    cube = product([halves(block) for block in square])
    for t in range(WIDE):
        value = 3.0 * square[t] - 2.0 * cube[t]
        for part in range(parts):
            out_ref[part ^ flip, t] = value[part * rows : (part + 1) * rows]


def shards(density, pattern):
    sizes = tuple(lax.axis_size(a) for a in AXES)
    cols, wide, rows, width = density.shape
    groups = [[owner(sizes, i + j) for j in range(cols)] for i in range(0, sizes[0] * sizes[1] * sizes[2], cols)]
    inside, outside = exchange(sizes, 0), exchange(sizes, 1)
    odd = place()[1] & 1

    def blocks(n):
        return jax.ShapeDtypeStruct((n, cols * rows, width), jnp.float32)

    parts = lax.all_to_all(density, AXES, 0, 0, axis_index_groups=groups, tiled=True)
    marks = jnp.pad(pattern.astype(jnp.float32), ((0, 0), (0, width - wide)))
    own, near, far = pl.pallas_call(
        arrange_kernel,
        out_shape=(blocks(wide), blocks(wide - 1), blocks(wide - 1)),
        in_specs=[VMEM] * 2,
        out_specs=(VMEM,) * 3,
        compiler_params=PARAMS,
    )(marks, parts)
    far = lax.ppermute(far, AXES, outside)
    near = lax.ppermute(near, AXES, inside)
    relayed = lax.ppermute(lax.dynamic_slice_in_dim(near, odd, wide - 2, 0), AXES, outside)
    handed = lax.ppermute(lax.dynamic_slice_in_dim(far, 1 - odd, wide - 2, 0), AXES, inside)
    result = pl.pallas_call(
        band_kernel,
        out_shape=jax.ShapeDtypeStruct(density.shape, jnp.float32),
        in_specs=[VMEM] * 6,
        out_specs=VMEM,
        compiler_params=PARAMS,
    )(marks, own, near, far, relayed, handed)
    return lax.all_to_all(result, AXES, 0, 0, axis_index_groups=groups, tiled=True)


def solution(mesh):
    in_specs = (P(("row", "depth"), None, "col", None), P(("row", "depth"), None))
    out_specs = P(("row", "depth"), None, "col", None)
    return jax.shard_map(shards, mesh=mesh, in_specs=in_specs, out_specs=out_specs, check_vma=False)
```

```python
import jax
import jax.numpy as jnp
from jax import lax
from jax.experimental import pallas as pl
from jax.experimental.pallas import tpu as pltpu
from jax.sharding import PartitionSpec as P

HALF = 2
WIDE = 5
AXES = ("row", "col", "depth")
START = 4
TURNED = 1
VMEM = pl.BlockSpec(memory_space=pltpu.VMEM)
PARAMS = pltpu.CompilerParams(vmem_limit_bytes=32 * 1024 * 1024)


def owner(sizes, i):
    rows, cols, depths = sizes
    chunk, at = divmod(i % (rows * cols * depths), cols)
    row, depth = divmod(chunk, depths)
    col = (START + (cols - 1 - at if chunk % 2 == TURNED else at)) % cols
    return (row * cols + col) * depths + depth


def exchange(sizes, first):
    result = []
    for i in range(first, sizes[0] * sizes[1] * sizes[2], 2):
        a, b = owner(sizes, i), owner(sizes, i + 1)
        result += [(a, b), (b, a)]
    return result


def place():
    cols = lax.axis_size("col")
    chunk = lax.axis_index("row") * lax.axis_size("depth") + lax.axis_index("depth")
    flip = jnp.where((chunk & 1) == TURNED, cols - 1, 0)
    return flip, ((lax.axis_index("col") + cols - START) % cols) ^ flip


def halves(value):
    high = value.astype(jnp.bfloat16)
    return high, (value - high.astype(jnp.float32)).astype(jnp.bfloat16)


def dot(left, right):
    return jnp.dot(left, right, preferred_element_type=jnp.float32)


def arrange_kernel(marks_ref, parts_ref, own_ref, near_ref, far_ref):
    parts, _, rows, _ = parts_ref.shape
    flip, row = place()
    odd = row & 1
    for slot in range(WIDE):
        keep = marks_ref[pl.ds(row, 1), slot : slot + 1]
        for part in range(parts):
            own_ref[slot, part * rows : (part + 1) * rows] = parts_ref[(part - START) % parts ^ flip, slot] * keep
    for slot in range(WIDE - 1):
        near_ref[slot] = own_ref[slot + 1 - odd]
        far_ref[slot] = own_ref[slot + odd]


def band_kernel(marks_ref, own_ref, near_ref, far_ref, relayed_ref, handed_ref, out_ref):
    parts, _, rows, _ = out_ref.shape
    flip, row = place()
    even = row & 1 == 0
    right = {(HALF, s): halves(own_ref[s]) for s in range(WIDE)}
    for s in range(WIDE - 1):
        near, far = near_ref[s], far_ref[s]
        right[HALF + 1, s] = halves(jnp.where(even, near, far))
        right[HALF - 1, s + 1] = halves(jnp.where(even, far, near))
    for s in range(WIDE - 2):
        relayed, handed = relayed_ref[s], handed_ref[s]
        right[HALF + 2, s] = halves(jnp.where(even, handed, relayed))
        right[HALF - 2, s + 2] = halves(jnp.where(even, relayed, handed))
    keep = [marks_ref[pl.ds(row, 1), t : t + 1] for t in range(WIDE)]

    def product(left):
        result = []
        for t in range(WIDE):
            summed = None
            for u in range(max(0, t - HALF), min(WIDE, t + HALF + 1)):
                high, low = left[u]
                other_high, other_low = right[u, t - u + HALF]
                term = dot(high, other_high) + dot(high, other_low) + dot(low, other_high)
                summed = term if summed is None else summed + term
            result.append(summed * keep[t])
        return result

    square = product([right[HALF, s] for s in range(WIDE)])
    cube = product([halves(block) for block in square])
    for t in range(WIDE):
        value = 3.0 * square[t] - 2.0 * cube[t]
        for part in range(parts):
            out_ref[(part - START) % parts ^ flip, t] = value[part * rows : (part + 1) * rows]


def shards(density, pattern):
    sizes = tuple(lax.axis_size(a) for a in AXES)
    cols, wide, rows, width = density.shape
    groups = [[owner(sizes, i + j) for j in range(cols)] for i in range(0, sizes[0] * sizes[1] * sizes[2], cols)]
    inside, outside = exchange(sizes, 0), exchange(sizes, 1)
    odd = place()[1] & 1

    def blocks(n):
        return jax.ShapeDtypeStruct((n, cols * rows, width), jnp.float32)

    parts = lax.all_to_all(density, AXES, 0, 0, axis_index_groups=groups, tiled=True)
    marks = jnp.pad(pattern.astype(jnp.float32), ((0, 0), (0, width - wide)))
    own, near, far = pl.pallas_call(
        arrange_kernel,
        out_shape=(blocks(wide), blocks(wide - 1), blocks(wide - 1)),
        in_specs=[VMEM] * 2,
        out_specs=(VMEM,) * 3,
        compiler_params=PARAMS,
    )(marks, parts)
    far = lax.ppermute(far, AXES, outside)
    near = lax.ppermute(near, AXES, inside)
    relayed = lax.ppermute(lax.dynamic_slice_in_dim(near, odd, wide - 2, 0), AXES, outside)
    handed = lax.ppermute(lax.dynamic_slice_in_dim(far, 1 - odd, wide - 2, 0), AXES, inside)
    result = pl.pallas_call(
        band_kernel,
        out_shape=jax.ShapeDtypeStruct(density.shape, jnp.float32),
        in_specs=[VMEM] * 6,
        out_specs=VMEM,
        compiler_params=PARAMS,
    )(marks, own, near, far, relayed, handed)
    return lax.all_to_all(result, AXES, 0, 0, axis_index_groups=groups, tiled=True)


def solution(mesh):
    in_specs = (P(("row", "depth"), None, "col", None), P(("row", "depth"), None))
    out_specs = P(("row", "depth"), None, "col", None)
    return jax.shard_map(shards, mesh=mesh, in_specs=in_specs, out_specs=out_specs, check_vma=False)
```

```python
import jax
import jax.numpy as jnp
from jax import lax
from jax.experimental import pallas as pl
from jax.experimental.pallas import tpu as pltpu
from jax.sharding import PartitionSpec as P

HALF = 2
WIDE = 5
AXES = ("row", "col", "depth")
START = 4
TURNED = 1
VMEM = pl.BlockSpec(memory_space=pltpu.VMEM)
PARAMS = pltpu.CompilerParams(vmem_limit_bytes=32 * 1024 * 1024)


def owner(sizes, i):
    rows, cols, depths = sizes
    chunk, at = divmod(i % (rows * cols * depths), cols)
    row, depth = divmod(chunk, depths)
    col = (START + (cols - 1 - at if chunk % 2 == TURNED else at)) % cols
    return (row * cols + col) * depths + depth


def exchange(sizes, first):
    result = []
    for i in range(first, sizes[0] * sizes[1] * sizes[2], 2):
        a, b = owner(sizes, i), owner(sizes, i + 1)
        result += [(a, b), (b, a)]
    return result


def place():
    cols = lax.axis_size("col")
    chunk = lax.axis_index("row") * lax.axis_size("depth") + lax.axis_index("depth")
    flip = jnp.where((chunk & 1) == TURNED, cols - 1, 0)
    return flip, ((lax.axis_index("col") + cols - START) % cols) ^ flip


def return_groups(sizes):
    rows, cols, depths = sizes
    return [
        [(row * cols + (START + j) % cols) * depths + depth for j in range(cols)]
        for row in range(rows)
        for depth in range(depths)
    ]


def halves(value):
    high = value.astype(jnp.bfloat16)
    return high, (value - high.astype(jnp.float32)).astype(jnp.bfloat16)


def dot(left, right):
    return jnp.dot(left, right, preferred_element_type=jnp.float32)


def arrange_kernel(marks_ref, parts_ref, own_ref, near_ref, far_ref):
    parts, _, rows, _ = parts_ref.shape
    flip, row = place()
    odd = row & 1
    for slot in range(WIDE):
        keep = marks_ref[pl.ds(row, 1), slot : slot + 1]
        for part in range(parts):
            own_ref[slot, part * rows : (part + 1) * rows] = parts_ref[(part - START) % parts ^ flip, slot] * keep
    for slot in range(WIDE - 1):
        near_ref[slot] = own_ref[slot + 1 - odd]
        far_ref[slot] = own_ref[slot + odd]


def band_kernel(marks_ref, own_ref, near_ref, far_ref, relayed_ref, handed_ref, out_ref):
    parts, _, rows, _ = out_ref.shape
    _, row = place()
    even = row & 1 == 0
    right = {(HALF, s): halves(own_ref[s]) for s in range(WIDE)}
    for s in range(WIDE - 1):
        near, far = near_ref[s], far_ref[s]
        right[HALF + 1, s] = halves(jnp.where(even, near, far))
        right[HALF - 1, s + 1] = halves(jnp.where(even, far, near))
    for s in range(WIDE - 2):
        relayed, handed = relayed_ref[s], handed_ref[s]
        right[HALF + 2, s] = halves(jnp.where(even, handed, relayed))
        right[HALF - 2, s + 2] = halves(jnp.where(even, relayed, handed))
    keep = [marks_ref[pl.ds(row, 1), t : t + 1] for t in range(WIDE)]

    def product(left):
        result = []
        for t in range(WIDE):
            summed = None
            for u in range(max(0, t - HALF), min(WIDE, t + HALF + 1)):
                high, low = left[u]
                other_high, other_low = right[u, t - u + HALF]
                term = dot(high, other_high) + dot(high, other_low) + dot(low, other_high)
                summed = term if summed is None else summed + term
            result.append(summed * keep[t])
        return result

    square = product([right[HALF, s] for s in range(WIDE)])
    cube = product([halves(block) for block in square])
    for t in range(WIDE):
        value = 3.0 * square[t] - 2.0 * cube[t]
        for part in range(parts):
            out_ref[(part - START) % parts, t] = value[part * rows : (part + 1) * rows]


def order_kernel(back_ref, out_ref, sems):
    flip, _ = place()
    copies = [
        pltpu.make_async_copy(back_ref.at[r ^ flip], out_ref.at[r], sems.at[r]) for r in range(out_ref.shape[0])
    ]
    for copy in copies:
        copy.start()
    for copy in copies:
        copy.wait()


def shards(density, pattern):
    sizes = tuple(lax.axis_size(a) for a in AXES)
    cols, wide, rows, width = density.shape
    groups = [[owner(sizes, i + j) for j in range(cols)] for i in range(0, sizes[0] * sizes[1] * sizes[2], cols)]
    inside, outside = exchange(sizes, 0), exchange(sizes, 1)
    odd = place()[1] & 1

    def blocks(n):
        return jax.ShapeDtypeStruct((n, cols * rows, width), jnp.float32)

    parts = lax.all_to_all(density, AXES, 0, 0, axis_index_groups=groups, tiled=True)
    marks = jnp.pad(pattern.astype(jnp.float32), ((0, 0), (0, width - wide)))
    own, near, far = pl.pallas_call(
        arrange_kernel,
        out_shape=(blocks(wide), blocks(wide - 1), blocks(wide - 1)),
        in_specs=[VMEM] * 2,
        out_specs=(VMEM,) * 3,
        compiler_params=PARAMS,
    )(marks, parts)
    far = lax.ppermute(far, AXES, outside)
    near = lax.ppermute(near, AXES, inside)
    relayed = lax.ppermute(lax.dynamic_slice_in_dim(near, odd, wide - 2, 0), AXES, outside)
    handed = lax.ppermute(lax.dynamic_slice_in_dim(far, 1 - odd, wide - 2, 0), AXES, inside)
    result = pl.pallas_call(
        band_kernel,
        out_shape=jax.ShapeDtypeStruct(density.shape, jnp.float32),
        in_specs=[VMEM] * 6,
        out_specs=VMEM,
        compiler_params=PARAMS,
    )(marks, own, near, far, relayed, handed)
    back = lax.all_to_all(result, AXES, 0, 0, axis_index_groups=return_groups(sizes), tiled=True)
    return pl.pallas_call(
        order_kernel,
        out_shape=jax.ShapeDtypeStruct(density.shape, jnp.float32),
        in_specs=[VMEM],
        out_specs=pl.BlockSpec(memory_space=pl.ANY),
        scratch_shapes=[pltpu.SemaphoreType.DMA((cols,))],
        compiler_params=PARAMS,
    )(back)


def solution(mesh):
    in_specs = (P(("row", "depth"), None, "col", None), P(("row", "depth"), None))
    out_specs = P(("row", "depth"), None, "col", None)
    return jax.shard_map(shards, mesh=mesh, in_specs=in_specs, out_specs=out_specs, check_vma=False)
```

```python
import jax
import jax.numpy as jnp
from jax import lax
from jax.experimental import pallas as pl
from jax.experimental.pallas import tpu as pltpu
from jax.sharding import PartitionSpec as P

HALF = 2
WIDE = 5
AXES = ("row", "col", "depth")
START = 4
VMEM = pl.BlockSpec(memory_space=pltpu.VMEM)
PARAMS = pltpu.CompilerParams(vmem_limit_bytes=32 * 1024 * 1024)


def owner(sizes, i):
    rows, cols, depths = sizes
    chunk, at = divmod(i % (rows * cols * depths), cols)
    row, depth = divmod(chunk, depths)
    return (row * cols + (START + at) % cols) * depths + depth


def exchange(sizes, first):
    result = []
    for i in range(first, sizes[0] * sizes[1] * sizes[2], 2):
        a, b = owner(sizes, i), owner(sizes, i + 1)
        result += [(a, b), (b, a)]
    return result


def own_row():
    cols = lax.axis_size("col")
    return (lax.axis_index("col") + cols - START) % cols


def halves(value):
    high = value.astype(jnp.bfloat16)
    return high, (value - high.astype(jnp.float32)).astype(jnp.bfloat16)


def dot(left, right):
    return jnp.dot(left, right, preferred_element_type=jnp.float32)


def arrange_kernel(marks_ref, parts_ref, own_ref, near_ref, far_ref):
    parts, _, rows, _ = parts_ref.shape
    row = own_row()
    odd = row & 1
    for slot in range(WIDE):
        keep = marks_ref[pl.ds(row, 1), slot : slot + 1]
        for part in range(parts):
            own_ref[slot, part * rows : (part + 1) * rows] = parts_ref[(part - START) % parts, slot] * keep
    for slot in range(WIDE - 1):
        near_ref[slot] = own_ref[slot + 1 - odd]
        far_ref[slot] = own_ref[slot + odd]


def band_kernel(marks_ref, own_ref, near_ref, far_ref, relayed_ref, handed_ref, out_ref):
    parts, _, rows, _ = out_ref.shape
    row = own_row()
    even = row & 1 == 0
    right = {(HALF, s): halves(own_ref[s]) for s in range(WIDE)}
    for s in range(WIDE - 1):
        near, far = near_ref[s], far_ref[s]
        right[HALF + 1, s] = halves(jnp.where(even, near, far))
        right[HALF - 1, s + 1] = halves(jnp.where(even, far, near))
    for s in range(WIDE - 2):
        relayed, handed = relayed_ref[s], handed_ref[s]
        right[HALF + 2, s] = halves(jnp.where(even, handed, relayed))
        right[HALF - 2, s + 2] = halves(jnp.where(even, relayed, handed))
    keep = [marks_ref[pl.ds(row, 1), t : t + 1] for t in range(WIDE)]

    def product(left):
        result = []
        for t in range(WIDE):
            summed = None
            for u in range(max(0, t - HALF), min(WIDE, t + HALF + 1)):
                high, low = left[u]
                other_high, other_low = right[u, t - u + HALF]
                term = dot(high, other_high) + dot(high, other_low) + dot(low, other_high)
                summed = term if summed is None else summed + term
            result.append(summed * keep[t])
        return result

    square = product([right[HALF, s] for s in range(WIDE)])
    cube = product([halves(block) for block in square])
    for t in range(WIDE):
        value = 3.0 * square[t] - 2.0 * cube[t]
        for part in range(parts):
            out_ref[(part - START) % parts, t] = value[part * rows : (part + 1) * rows]


def shards(density, pattern):
    sizes = tuple(lax.axis_size(a) for a in AXES)
    cols, wide, rows, width = density.shape
    groups = [[owner(sizes, i + j) for j in range(cols)] for i in range(0, sizes[0] * sizes[1] * sizes[2], cols)]
    inside, outside = exchange(sizes, 0), exchange(sizes, 1)
    odd = own_row() & 1

    def blocks(n):
        return jax.ShapeDtypeStruct((n, cols * rows, width), jnp.float32)

    parts = lax.all_to_all(density, AXES, 0, 0, axis_index_groups=groups, tiled=True)
    marks = jnp.pad(pattern.astype(jnp.float32), ((0, 0), (0, width - wide)))
    own, near, far = pl.pallas_call(
        arrange_kernel,
        out_shape=(blocks(wide), blocks(wide - 1), blocks(wide - 1)),
        in_specs=[VMEM] * 2,
        out_specs=(VMEM,) * 3,
        compiler_params=PARAMS,
    )(marks, parts)
    far = lax.ppermute(far, AXES, outside)
    near = lax.ppermute(near, AXES, inside)
    relayed = lax.ppermute(lax.dynamic_slice_in_dim(near, odd, wide - 2, 0), AXES, outside)
    handed = lax.ppermute(lax.dynamic_slice_in_dim(far, 1 - odd, wide - 2, 0), AXES, inside)
    result = pl.pallas_call(
        band_kernel,
        out_shape=jax.ShapeDtypeStruct(density.shape, jnp.float32),
        in_specs=[VMEM] * 6,
        out_specs=VMEM,
        compiler_params=PARAMS,
    )(marks, own, near, far, relayed, handed)
    return lax.all_to_all(result, AXES, 0, 0, axis_index_groups=groups, tiled=True)


def solution(mesh):
    in_specs = (P(("row", "depth"), None, "col", None), P(("row", "depth"), None))
    out_specs = P(("row", "depth"), None, "col", None)
    return jax.shard_map(shards, mesh=mesh, in_specs=in_specs, out_specs=out_specs, check_vma=False)
```
